32 devices in a mesh: section: 2 (over core), expert: 16 (over z, y, x).
Axes of the slice: x: 2, y: 2, z: 4, core: 2. Of those that a mesh axis runs over, the one named last changes fastest.
Arguments:
- tokens: bfloat16 [2, 4096, 1024], P('section', 'expert'), may hold values from -6 to 6
- gates: float32 [2, 4096], P('section', 'expert'), may hold values from 0.2 to 1
- routes: int32 [2, 4096, 1], P('section', 'expert'), may hold values from 0 to 15; in each aligned block of 256 rows (0 to 255, 256 to 511, ..., all dimensions but the last counted through in order) at most 32 rows name the same one
- capacity: int32 [2, 16], P('section', 'expert'), may hold values from 128 to 512
- mem_lengths: int32 [2, 16], P('section', 'expert'), may hold values from 64 to 256
- mem_keys: bfloat16 [2, 2048, 1024], P('section', 'expert')
- mem_values: bfloat16 [2, 2048, 1024], P('section', 'expert'), may hold values from -6 to 6
- q_weight: bfloat16 [2, 1024, 1024], P('section', 'expert'), may hold values from -0.1875 to 0.1875
- out_weight: bfloat16 [2, 1024, 1024], P('section', 'expert'), may hold values from -0.75 to 0.75
- w_in: bfloat16 [2, 16, 1024, 1408], P('section', 'expert'), may hold values from -0.1875 to 0.1875
Outputs:
- expert_hidden: bfloat16 [2, 4096, 1408], P('section', 'expert')
The draws below stay inside these ranges and needn't reach their ends.
Inputs may be any that keep to these rules, and one draw needn't show every extreme that they name: `routes`: among the 256 rows of one device at most 32 name one expert.
All inputs are finite; a program needn't handle non-finite values.
Results may differ from the reference program's by a relative error of at most 0.013.
Values may be sent and summed in bfloat16 or wider, within the bound.
A program may use at most 64 MiB of HBM per device.

```python
import math
import jax
import jax.numpy as jnp
import numpy as np
from jax import lax

D = 1024
HEADS = 16
HEAD_DIM = 64
HID = 1408
TOK_DEV = 256
MEM_LEN = 256
MEM_HALF = 128
EXPERTS = 16
CAP_SRC = 32
TOKENS = 4096
MEM_ROWS = 2048
N_SECTION = 2
N_EXPERT = 16


def draw_mem_keys(key, part):
    first = jax.random.fold_in(key, 0)
    base = jax.random.normal(first, (N_SECTION, MEM_ROWS, D), jnp.float32)
    return base.astype(jnp.bfloat16)


def with_ends(result, stream_key, least, high):
    extent = result.shape
    index_at = [jax.random.randint(jax.random.fold_in(stream_key, axis), (), 0, extent[axis]) for axis in range(len(extent))]
    result = result.at[tuple(index_at)].set(least)
    longest = extent.index(max(extent))
    index_at[longest] = (index_at[longest] + 1) % extent[longest]
    return result.at[tuple(index_at)].set(high)


def block_levels(stream_key, extent, pieces, smallest, high):
    def one(dim, parts):
        heights = jax.random.uniform(jax.random.fold_in(jax.random.fold_in(stream_key, 6), dim), (parts,), jnp.float32, smallest / len(pieces), high / len(pieces))
        return jnp.repeat(jnp.exp(heights), extent[dim] // parts).reshape((-1,) + (1,) * (len(extent) - dim - 1))

    loudness = one(*pieces[0])
    for cut in pieces[1:]:
        loudness = loudness * one(*cut)
    return loudness


def assign_block(own_key, own, number, rows, number_of, top, bound, slope):
    order = jax.random.permutation(own_key, number_of)
    packed, ordinary = shares(number_of, rows * top, bound, slope, True), shares(number_of, rows * top, bound, slope, False)
    places = jnp.arange(number_of)

    def named(tallies, turn):
        used = int((tallies > 0).sum())
        fixed = max(1, used // 4)
        passed = fixed + (places - fixed + turn * (used - fixed)) % max(1, number_of - fixed)
        return jnp.zeros((number_of,), jnp.int32).at[order[jnp.where(places < fixed, places, passed)]].set(jnp.asarray(tallies, jnp.int32))

    tallies = jnp.where(number % 4 == 0, named(packed, number // 4), named(ordinary, number - number // 4 - 1))
    mixed = jax.random.permutation(jax.random.fold_in(own, 3), number_of)
    donor, taker = mixed[0:number_of // 2 * 2:2], mixed[1:number_of // 2 * 2:2]
    slack = jnp.minimum(tallies[donor] - 1, bound - tallies[taker]) // 2
    slack = jnp.where((donor == order[0]) | (taker == order[0]) | (tallies[taker] == 0), 0, jnp.maximum(slack, 0))
    passed = jax.random.randint(jax.random.fold_in(own, 4), (number_of // 2,), 0, 1 << 20) % (slack + 1)
    tallies = tallies.at[donor].add(-passed).at[taker].add(passed)
    labels = jnp.searchsorted(jnp.cumsum(tallies), jnp.arange(rows * top), side="right").astype(jnp.int32)
    table = labels.reshape(top, rows).T
    table = table[jax.random.permutation(jax.random.fold_in(own, 1), rows)]
    turn = jax.random.randint(jax.random.fold_in(own, 2), (rows, 1), 0, top)
    return jnp.take_along_axis(table, (jnp.arange(top)[None, :] + turn) % top, axis=1)


def shares(count, total, most, skew, full):
    portions = [(1 << 20) // math.isqrt(grade ** skew) + 1 for grade in range(1, count + 1)]
    largest = most if full else min(most, max(-(-total // count), total * portions[0] // sum(portions)))
    least = 1 if total - largest >= count - 1 else 0
    holding, rest = [largest] + [least] * (count - 1), total - largest - least * (count - 1)
    while rest > 0:
        free = [i for i in range(1, count) if holding[i] < largest] or [i for i in range(1, count) if holding[i] < most]
        pool, budget = sum([portions[i] for i in free]), rest
        for i in free:
            extra = min(most - holding[i], max(1, budget * portions[i] // pool), rest)
            holding[i] = holding[i] + extra
            rest = rest - extra
    return np.array(holding)


def bell_draw(stream_key, dims, spread, bound, cuts=(), kind=jnp.bfloat16):
    entries = spread * jax.random.normal(stream_key, dims, jnp.float32)
    if cuts:
        entries = entries * block_levels(stream_key, dims, cuts, -0.22, 0.18)
    return jnp.clip(entries, -bound, bound).astype(kind)


def setup_inputs(seed: int = 0) -> dict:
    arg_keys = jax.random.split(jax.random.key(seed), 11)
    tokens = bell_draw(arg_keys[0], (N_SECTION, TOKENS, D), 1.0, 6.0, ((0, 2), (1, 16)))
    gates = jnp.clip(jnp.exp(math.log(1.0) - 1.609438 * jax.random.uniform(arg_keys[1], (N_SECTION, TOKENS), jnp.float32) ** block_levels(arg_keys[1], (N_SECTION, TOKENS), ((0, 2), (1, 16)), -0.2, 0.2)), 0.2, 1.0)
    routes_keys = jax.random.split(jax.random.fold_in(arg_keys[2], 1), N_SECTION * TOKENS // TOK_DEV)
    routes_turns = jax.random.permutation(jax.random.fold_in(arg_keys[2], 3), N_SECTION * TOKENS // TOK_DEV)
    routes = jax.vmap(lambda own, number: assign_block(jax.random.fold_in(arg_keys[2], 2), own, number, TOK_DEV, EXPERTS, 1, CAP_SRC, 2))(routes_keys, routes_turns).reshape((N_SECTION, TOKENS, 1))
    capacity = with_ends(jax.random.randint(arg_keys[3], (N_SECTION, EXPERTS), TOK_DEV // 2, 2 * TOK_DEV + 1), jax.random.fold_in(arg_keys[3], 1), TOK_DEV // 2, 2 * TOK_DEV).astype(jnp.int32)
    mem_lengths = with_ends(jax.random.randint(arg_keys[4], (N_SECTION, N_EXPERT), MEM_LEN // 4, MEM_LEN + 1), jax.random.fold_in(arg_keys[4], 1), MEM_LEN // 4, MEM_LEN).astype(jnp.int32)
    mem_keys = draw_mem_keys(jax.random.fold_in(arg_keys[10], 71), 0)
    mem_values = bell_draw(arg_keys[6], (N_SECTION, MEM_ROWS, D), 1.0, 6.0, ((0, 2), (1, 16)))
    q_weight = bell_draw(arg_keys[7], (N_SECTION, D, D), D ** -0.5, 0.1875, ((0, 2), (1, 16)))
    out_weight = bell_draw(arg_keys[8], (N_SECTION, D, D), (D // 16) ** -0.5, 0.75, ((0, 2), (1, 16)))
    w_in = bell_draw(arg_keys[9], (N_SECTION, EXPERTS, D, HID), D ** -0.5, 0.1875, ((0, 2), (1, 16)))
    return {"tokens": tokens, "gates": gates, "routes": routes, "capacity": capacity, "mem_lengths": mem_lengths, "mem_keys": mem_keys, "mem_values": mem_values, "q_weight": q_weight, "out_weight": out_weight, "w_in": w_in}


def attend(query, keys, values, length):
    qh = query.reshape(TOK_DEV, HEADS, HEAD_DIM).astype(jnp.float32)
    kh = keys.reshape(MEM_LEN, HEADS, HEAD_DIM).astype(jnp.float32)
    vh = values.reshape(MEM_LEN, HEADS, HEAD_DIM).astype(jnp.float32)
    scores = jnp.einsum('qhd,khd->hqk', qh, kh) / jnp.sqrt(jnp.float32(HEAD_DIM))
    valid = jnp.arange(MEM_LEN, dtype=jnp.int32) < length
    scores = jnp.where(valid[None, None, :], scores, jnp.float32(-1e+30))
    scores = scores - lax.optimization_barrier(jnp.max(scores, axis=-1, keepdims=True))
    weights = jnp.exp(scores)
    probs = (weights / lax.optimization_barrier(jnp.sum(weights, axis=-1, keepdims=True))).astype(jnp.bfloat16)
    context = jnp.einsum('hqk,khd->qhd', probs.astype(jnp.float32), vh)
    return context.reshape(TOK_DEV, D).astype(jnp.bfloat16)

def reference(tokens, gates, routes, capacity, mem_lengths, mem_keys, mem_values, q_weight, out_weight, w_in):
    half = N_SECTION // 2
    results = []
    for section in range(N_SECTION):
        inputs = tokens[section]
        if section >= half:
            query = jnp.dot(inputs, q_weight[section], preferred_element_type=jnp.float32).astype(jnp.bfloat16)
            keys = jnp.concatenate([mem_keys[section - half].reshape(N_EXPERT, MEM_HALF, D), mem_keys[section].reshape(N_EXPERT, MEM_HALF, D)], axis=1)
            values = jnp.concatenate([mem_values[section - half].reshape(N_EXPERT, MEM_HALF, D), mem_values[section].reshape(N_EXPERT, MEM_HALF, D)], axis=1)
            context = lax.map(lambda item: attend(item[0], item[1], item[2], item[3]), (query.reshape(N_EXPERT, TOK_DEV, D), keys, values, mem_lengths[section]))
            context = context.reshape(TOKENS, D)
            attn_out = jnp.dot(context, out_weight[section], preferred_element_type=jnp.float32)
            mixed = (inputs.astype(jnp.float32) + attn_out).astype(jnp.bfloat16)
        else:
            mixed = inputs
        route = routes[section][:, 0].astype(jnp.int32)
        onehot = (route[:, None] == jnp.arange(EXPERTS, dtype=jnp.int32)[None, :]).astype(jnp.int32)
        grank = lax.optimization_barrier(jnp.sum((jnp.cumsum(onehot, axis=0) - onehot) * onehot, axis=1))
        kept = (grank < capacity[section][route]).astype(jnp.float32)
        local_hot = onehot.reshape(N_EXPERT, TOK_DEV, EXPERTS)
        lrank = lax.optimization_barrier(jnp.sum((jnp.cumsum(local_hot, axis=1) - local_hot) * local_hot, axis=2)).reshape(TOKENS)
        source = jnp.arange(TOKENS, dtype=jnp.int32) // TOK_DEV
        slot = (source * CAP_SRC + lrank).astype(jnp.int32)
        buffer = jnp.zeros((EXPERTS, N_EXPERT * CAP_SRC, D), jnp.bfloat16).at[route, slot].set(mixed)
        acts = lax.map(lambda item: jnp.maximum(jnp.dot(item[0], item[1], preferred_element_type=jnp.float32), 0.0).astype(jnp.bfloat16), (buffer, w_in[section]))
        picked = acts[route, slot].astype(jnp.float32)
        results.append((picked * gates[section][:, None] * kept[:, None]).astype(jnp.bfloat16))
    return jnp.stack(results, axis=0)
```

```python
import functools

import jax
import jax.numpy as jnp
from jax import lax
from jax.experimental import pallas as pl
from jax.experimental.pallas import tpu as pltpu
from jax.sharding import PartitionSpec as P

HEADS = 16
LANES = 128
PLANE = 4
MESH = pl.DeviceIdType.MESH
F32 = jnp.float32
BF16 = jnp.bfloat16


def relay(
    sections, experts, cap,
    tokens, gates, routes, capacity, lengths, mem_k, mem_v, q_in, o_in, w_hbm,
    out,
    w_vmem, wbuf, kbuf, vbuf, qbuf, cbuf, mixed, buf, recv, acts, back, acc, cnt,
    local_sem, kv_send, kv_recv, w_send, w_recv,
    cnt_send, cnt_recv, fwd_send, fwd_recv, ret_send, ret_recv,
):
    half = sections // 2
    planes = experts // PLANE
    tok = tokens.shape[1]
    width = tokens.shape[2]
    span = mem_k.shape[1]
    shard = q_in.shape[1]
    rows = PLANE * cap
    sec = lax.axis_index("section")
    me = lax.axis_index("expert")
    a, j = me // PLANE, me % PLANE
    jy, jx = j // 2, j % 2
    by_x = jy * 2 + (1 - jx)
    by_y = (1 - jy) * 2 + jx
    decoding = sec >= half
    pair = lax.rem(sec + half, sections)

    def remote(src, dst, send, recv_sem, section, peer):
        return pltpu.make_async_remote_copy(
            src_ref=src, dst_ref=dst, send_sem=send, recv_sem=recv_sem,
            device_id=(section, peer), device_id_type=MESH,
        )

    get_w = pltpu.make_async_copy(w_hbm.at[0, 0], w_vmem, local_sem.at[0])
    get_w.start()
    own_rows = pl.ds(me * shard, shard)
    own = [
        pltpu.make_async_copy(q_in.at[0], wbuf.at[0, own_rows], local_sem.at[1]),
        pltpu.make_async_copy(o_in.at[0], wbuf.at[1, own_rows], local_sem.at[2]),
        pltpu.make_async_copy(mem_k.at[0], kbuf.at[pl.ds(span, span)], local_sem.at[3]),
        pltpu.make_async_copy(mem_v.at[0], vbuf.at[pl.ds(span, span)], local_sem.at[4]),
    ]

    @pl.when(decoding)
    def _():
        for copy in own:
            copy.start()

    barrier = pltpu.get_barrier_semaphore()

    def greet(k, carry):
        pl.semaphore_signal(
            barrier, inc=1, device_id=(sec, lax.rem(me + k, experts)), device_id_type=MESH
        )
        return carry

    lax.fori_loop(1, experts, greet, 0)
    pl.semaphore_signal(barrier, inc=1, device_id=(pair, me), device_id_type=MESH)
    pl.semaphore_wait(barrier, experts)

    kv = [
        remote(mem_k.at[0], kbuf.at[pl.ds(0, span)], kv_send.at[0], kv_recv.at[0], pair, me),
        remote(mem_v.at[0], vbuf.at[pl.ds(0, span)], kv_send.at[1], kv_recv.at[1], pair, me),
    ]
    first = (by_x, by_y)
    second = (by_y, by_x)

    def w_copy(kind, hop, plane, owner, peer, from_input=False):
        span_ = pl.ds(owner * shard, shard)
        src = (q_in, o_in)[kind].at[0] if from_input else wbuf.at[kind, span_]
        return remote(
            src, wbuf.at[kind, span_], w_send.at[kind, hop, plane], w_recv.at[kind, owner], sec, peer
        )

    @pl.when(jnp.logical_not(decoding))
    def _():
        for copy in kv:
            copy.start()

    @pl.when(decoding)
    def _():
        for kind in range(2):
            def to_planes(dz, carry):
                w_copy(kind, 0, dz, me, lax.rem(a + dz, planes) * PLANE + j, True).start()
                return carry

            lax.fori_loop(1, planes, to_planes, 0)
            w_copy(kind, 1, 0, me, a * PLANE + first[kind], True).start()
            w_copy(kind, 2, 0, me, a * PLANE + second[kind], True).start()

    eye = lax.broadcasted_iota(jnp.int32, (tok, tok), 0) == lax.broadcasted_iota(
        jnp.int32, (tok, tok), 1
    )
    earlier = lax.broadcasted_iota(jnp.int32, (tok, tok), 1) < lax.broadcasted_iota(
        jnp.int32, (tok, tok), 0
    )
    lane = lax.broadcasted_iota(jnp.int32, (tok, LANES), 1).astype(F32)
    route_row = routes[...].astype(F32)
    route_col = jnp.sum(jnp.where(eye, route_row, 0.0), axis=1, keepdims=True)
    gate_col = jnp.sum(jnp.where(eye, gates[...], 0.0), axis=1, keepdims=True)
    onehot = jnp.where(lane == route_col, 1.0, 0.0)
    before = jnp.dot(
        jnp.where(earlier, 1.0, 0.0).astype(BF16), onehot.astype(BF16), preferred_element_type=F32
    )
    lrank = jnp.sum(before * onehot, axis=1, keepdims=True)
    slot_col = route_col * cap + lrank
    slot_row = jnp.sum(jnp.where(eye, slot_col, 0.0), axis=0, keepdims=True)
    cnt[me] = jnp.broadcast_to(jnp.sum(onehot, axis=0, keepdims=True), (8, LANES))

    def cnt_copy(k):
        peer = lax.rem(me + k, experts)
        return remote(cnt.at[me], cnt.at[me], cnt_send.at[k], cnt_recv.at[me], sec, peer)

    def cnt_start(k, carry):
        cnt_copy(k).start()
        return carry

    lax.fori_loop(1, experts, cnt_start, 0)

    @pl.when(jnp.logical_not(decoding))
    def _():
        mixed[...] = tokens[0]

    @pl.when(decoding)
    def _():
        def from_planes(dz, carry):
            plane = lax.rem(a - dz + planes, planes)
            owner = plane * PLANE + j
            for kind in range(2):
                w_copy(kind, 0, dz, owner, owner).wait_recv()
                w_copy(kind, 1, dz, owner, a * PLANE + first[kind]).start()
                w_copy(kind, 2, dz, owner, a * PLANE + second[kind]).start()
            return carry

        lax.fori_loop(1, planes, from_planes, 0)

        def pass_on(dz, carry):
            plane = lax.rem(a - dz + planes, planes)
            for kind in range(2):
                owner = plane * PLANE + first[kind]
                w_copy(kind, 1, dz, owner, a * PLANE + first[kind]).wait_recv()
                w_copy(kind, 3, dz, owner, a * PLANE + second[kind]).start()
            return carry

        lax.fori_loop(0, planes, pass_on, 0)

        def arrive(kind):
            def body(dz, carry):
                plane = lax.rem(a - dz + planes, planes)
                for hop, jj in ((2, second[kind]), (3, 3 - j)):
                    w_copy(kind, hop, dz, plane * PLANE + jj, a * PLANE + second[kind]).wait_recv()
                return carry

            lax.fori_loop(0, planes, body, 0)

        own[0].wait()
        arrive(0)
        tile = 256

        @pl.loop(0, width // tile)
        def _(n):
            cols = pl.ds(pl.multiple_of(n * tile, tile), tile)
            qbuf[:, cols] = jnp.dot(
                tokens[0], wbuf[0, :, cols], preferred_element_type=F32
            ).astype(BF16)

        own[2].wait()
        own[3].wait()
        for copy in kv:
            copy.wait_recv()
        head_dim = width // HEADS
        length = lengths[0, 0]
        valid = lax.broadcasted_iota(jnp.int32, (tok, 2 * span), 1) < length
        low = lax.broadcasted_iota(jnp.int32, (tok, 2 * head_dim), 1) < head_dim
        mask_low = jnp.where(low, 1.0, 0.0).astype(BF16)
        mask_high = jnp.where(low, 0.0, 1.0).astype(BF16)
        scale = 1.0 / (head_dim ** 0.5)

        @pl.loop(0, HEADS // 2)
        def _(i):
            cols = pl.ds(pl.multiple_of(i * 2 * head_dim, 2 * head_dim), 2 * head_dim)
            q2, k2, v2 = qbuf[:, cols], kbuf[:, cols], vbuf[:, cols]
            parts = []
            for mask in (mask_low, mask_high):
                scores = lax.dot_general(
                    q2 * mask, k2, (((1,), (1,)), ((), ())), preferred_element_type=F32
                ) * scale
                scores = jnp.where(valid, scores, -1e30)
                scores = scores - jnp.max(scores, axis=-1, keepdims=True)
                weights = jnp.exp(scores)
                probs = (weights / jnp.sum(weights, axis=-1, keepdims=True)).astype(BF16)
                parts.append(jnp.dot(probs, v2, preferred_element_type=F32))
            cbuf[:, cols] = jnp.where(low, parts[0], parts[1]).astype(BF16)

        own[1].wait()
        arrive(1)

        @pl.loop(0, width // tile)
        def _(n):
            cols = pl.ds(pl.multiple_of(n * tile, tile), tile)
            attn = jnp.dot(cbuf[...], wbuf[1, :, cols], preferred_element_type=F32)
            mixed[:, cols] = (tokens[0, :, cols].astype(F32) + attn).astype(BF16)

    def block(index):
        return pl.ds(pl.multiple_of(index * cap, cap), cap)

    def fwd_copy(peer):
        return remote(
            buf.at[block(peer)], recv.at[block(me)], fwd_send.at[peer], fwd_recv.at[me], sec, peer
        )

    def fwd_arrival(src):
        return remote(
            buf.at[block(src)], recv.at[block(src)], fwd_send.at[src], fwd_recv.at[src], sec, src
        )

    def ret_copy(peer):
        return remote(
            acts.at[block(peer)], back.at[block(me)], ret_send.at[peer], ret_recv.at[me], sec, peer
        )

    def ret_arrival(src):
        return remote(
            acts.at[block(src)], back.at[block(src)], ret_send.at[src], ret_recv.at[src], sec, src
        )

    def in_plane(plane, visit):
        for s in range(PLANE):
            peer = plane * PLANE + lax.rem(j + s, PLANE)
            if s > 0:
                visit(peer)
            else:
                @pl.when(plane != a)
                def _():
                    visit(peer)

    def group(plane):
        return pl.ds(pl.multiple_of(plane * rows, rows), rows)

    def dispatch(dz, carry):
        plane = lax.rem(a + dz, planes)
        at = (lax.broadcasted_iota(jnp.int32, (rows, tok), 0) + plane * rows).astype(F32)
        placing = jnp.where(slot_row == at, 1.0, 0.0).astype(BF16)
        buf[group(plane), :] = jnp.dot(placing, mixed[...], preferred_element_type=F32).astype(BF16)
        in_plane(plane, lambda peer: fwd_copy(peer).start())
        return carry

    lax.fori_loop(0, planes, dispatch, 0)
    recv[block(me), :] = buf[block(me), :]

    def cnt_wait(k, carry):
        src = lax.rem(me + k, experts)
        remote(cnt.at[src], cnt.at[src], cnt_send.at[k], cnt_recv.at[src], sec, src).wait_recv()
        return carry

    lax.fori_loop(1, experts, cnt_wait, 0)
    get_w.wait()
    counts = cnt[:, 0, :].astype(BF16)
    limit = capacity[0, 0].astype(F32)

    def expert(dz, carry):
        plane = lax.rem(a - dz + planes, planes)
        in_plane(plane, lambda src: fwd_arrival(src).wait_recv())
        act = jnp.maximum(
            jnp.dot(recv[group(plane), :], w_vmem[...], preferred_element_type=F32), 0.0
        )
        row = lax.broadcasted_iota(jnp.int32, (rows, experts), 0)
        source = lax.broadcasted_iota(jnp.int32, (rows, experts), 1)
        lower = jnp.where(source < plane * PLANE + row // cap, 1.0, 0.0).astype(BF16)
        sums = jnp.dot(lower, counts, preferred_element_type=F32)
        mine = lax.broadcasted_iota(jnp.int32, (rows, LANES), 1) == me
        offset = jnp.sum(jnp.where(mine, sums, 0.0), axis=1, keepdims=True)
        rank = offset + (lax.broadcasted_iota(jnp.int32, (rows, 1), 0) % cap).astype(F32)
        kept = jnp.where(rank < limit, 1.0, 0.0)
        acts[group(plane), :] = (act * kept).astype(BF16)
        in_plane(plane, lambda peer: ret_copy(peer).start())
        return carry

    lax.fori_loop(0, planes, expert, 0)
    back[block(me), :] = acts[block(me), :]
    acc[...] = jnp.zeros_like(acc)

    def combine(dz, carry):
        plane = lax.rem(a - dz + planes, planes)
        in_plane(plane, lambda src: ret_arrival(src).wait_recv())
        at = (lax.broadcasted_iota(jnp.int32, (tok, rows), 1) + plane * rows).astype(F32)
        placing = jnp.where(slot_col == at, 1.0, 0.0).astype(BF16)
        acc[...] += jnp.dot(placing, back[group(plane), :], preferred_element_type=F32)
        return carry

    lax.fori_loop(0, planes, combine, 0)
    out[0] = (acc[...] * gate_col).astype(BF16)

    def sent(k, carry):
        peer = lax.rem(me + k, experts)
        cnt_copy(k).wait_send()
        fwd_copy(peer).wait_send()
        ret_copy(peer).wait_send()
        return carry

    lax.fori_loop(1, experts, sent, 0)

    @pl.when(jnp.logical_not(decoding))
    def _():
        for copy in kv:
            copy.wait_send()

    @pl.when(decoding)
    def _():
        for kind in range(2):
            def w_sent(dz, carry):
                for hop in range(4):
                    def done():
                        w_copy(kind, hop, dz, me, a * PLANE + second[kind]).wait_send()

                    if hop == 0:
                        pl.when(dz > 0)(done)
                    else:
                        done()
                return carry

            lax.fori_loop(0, planes, w_sent, 0)


def shards(
    tokens, gates, routes, capacity, mem_lengths, mem_keys, mem_values, q_weight, out_weight, w_in
):
    sections = lax.axis_size("section")
    experts = lax.axis_size("expert")
    tok, width = tokens.shape[1:]
    hidden = w_in.shape[3]
    span = mem_keys.shape[1]
    cap = max(16, 2 * tok // experts)
    slots = experts * cap
    planes = experts // PLANE
    dma = pltpu.SemaphoreType.DMA
    vmem = pl.BlockSpec(memory_space=pltpu.VMEM)
    smem = pl.BlockSpec(memory_space=pltpu.SMEM)
    hbm = pl.BlockSpec(memory_space=pl.ANY)
    return pl.pallas_call(
        functools.partial(relay, sections, experts, cap),
        out_shape=jax.ShapeDtypeStruct((1, tok, hidden), BF16),
        in_specs=[vmem, vmem, vmem, smem, smem, hbm, hbm, hbm, hbm, hbm],
        out_specs=vmem,
        scratch_shapes=[
            pltpu.VMEM((width, hidden), BF16),
            pltpu.VMEM((2, width, width), BF16),
            pltpu.VMEM((2 * span, width), BF16),
            pltpu.VMEM((2 * span, width), BF16),
            pltpu.VMEM((tok, width), BF16),
            pltpu.VMEM((tok, width), BF16),
            pltpu.VMEM((tok, width), BF16),
            pltpu.VMEM((slots, width), BF16),
            pltpu.VMEM((slots, width), BF16),
            pltpu.VMEM((slots, hidden), BF16),
            pltpu.VMEM((slots, hidden), BF16),
            pltpu.VMEM((tok, hidden), F32),
            pltpu.VMEM((experts, 8, LANES), F32),
            dma((5,)),
            dma((2,)),
            dma((2,)),
            dma((2, 4, planes)),
            dma((2, experts)),
            dma((experts,)),
            dma((experts,)),
            dma((experts,)),
            dma((experts,)),
            dma((experts,)),
            dma((experts,)),
        ],
        compiler_params=pltpu.CompilerParams(
            collective_id=0, has_side_effects=True, vmem_limit_bytes=48 * 1024 * 1024
        ),
        cost_estimate=pl.CostEstimate(
            flops=4 * tok * width * width + 2 * slots * width * hidden,
            bytes_accessed=2 * width * hidden + 8 * width * width,
            transcendentals=HEADS * tok * 2 * span,
        ),
    )(
        tokens, gates, routes.reshape(1, tok), capacity, mem_lengths,
        mem_keys, mem_values, q_weight, out_weight, w_in,
    )


def solution(mesh):
    in_specs = (
        P("section", "expert", None),
        P("section", "expert"),
        P("section", "expert", None),
        P("section", "expert"),
        P("section", "expert"),
        P("section", "expert", None),
        P("section", "expert", None),
        P("section", "expert", None),
        P("section", "expert", None),
        P("section", "expert", None, None),
    )
    out_specs = P("section", "expert", None)
    return jax.shard_map(shards, mesh=mesh, in_specs=in_specs, out_specs=out_specs, check_vma=False)
```

```python
import functools

import jax
import jax.numpy as jnp
from jax import lax
from jax.experimental import pallas as pl
from jax.experimental.pallas import tpu as pltpu
from jax.sharding import PartitionSpec as P

HEADS = 16
LANES = 128
PLANE = 4
MESH = pl.DeviceIdType.MESH
F32 = jnp.float32
BF16 = jnp.bfloat16


def relay(
    sections, experts, cap,
    tokens, gates, routes, capacity, lengths, mem_k, mem_v, q_in, o_in, w_hbm,
    out,
    w_vmem, tok_vmem, wbuf, kbuf, vbuf, qbuf, cbuf, mixed, buf, recv, acts, back, acc, cnt,
    turn, local_sem, kv_send, kv_recv, w_send, w_recv,
    cnt_send, cnt_recv, fwd_send, fwd_recv, ret_send, ret_recv,
):
    half = sections // 2
    planes = experts // PLANE
    tok = tokens.shape[1]
    width = tokens.shape[2]
    span = mem_k.shape[1]
    shard = q_in.shape[1]
    rows = PLANE * cap
    sec = lax.axis_index("section")
    me = lax.axis_index("expert")
    a, j = me // PLANE, me % PLANE
    jy, jx = j // 2, j % 2
    by_x = jy * 2 + (1 - jx)
    by_y = (1 - jy) * 2 + jx
    decoding = sec >= half
    pair = lax.rem(sec + half, sections)

    def remote(src, dst, send, recv_sem, section, peer):
        return pltpu.make_async_remote_copy(
            src_ref=src, dst_ref=dst, send_sem=send, recv_sem=recv_sem,
            device_id=(section, peer), device_id_type=MESH,
        )

    get_w = pltpu.make_async_copy(w_hbm.at[0, 0], w_vmem, local_sem.at[0])
    get_w.start()
    to_mixed = pltpu.make_async_copy(tokens.at[0], mixed, local_sem.at[5])
    to_vmem = pltpu.make_async_copy(tokens.at[0], tok_vmem, local_sem.at[5])
    own_rows = pl.ds(me * shard, shard)
    own = [
        pltpu.make_async_copy(q_in.at[0], wbuf.at[0, own_rows], local_sem.at[1]),
        pltpu.make_async_copy(o_in.at[0], wbuf.at[1, own_rows], local_sem.at[2]),
        pltpu.make_async_copy(mem_k.at[0], kbuf.at[pl.ds(span, span)], local_sem.at[3]),
        pltpu.make_async_copy(mem_v.at[0], vbuf.at[pl.ds(span, span)], local_sem.at[4]),
    ]

    @pl.when(jnp.logical_not(decoding))
    def _():
        to_mixed.start()

    @pl.when(decoding)
    def _():
        to_vmem.start()
        for copy in own:
            copy.start()

    barrier = pltpu.get_barrier_semaphore()

    def greet(k, carry):
        pl.semaphore_signal(
            barrier, inc=1, device_id=(sec, lax.rem(me + k, experts)), device_id_type=MESH
        )
        return carry

    lax.fori_loop(1, experts, greet, 0)
    pl.semaphore_signal(barrier, inc=1, device_id=(pair, me), device_id_type=MESH)
    pl.semaphore_wait(barrier, experts)

    kv = [
        remote(mem_k.at[0], kbuf.at[pl.ds(0, span)], kv_send.at[0], kv_recv.at[0], pair, me),
        remote(mem_v.at[0], vbuf.at[pl.ds(0, span)], kv_send.at[1], kv_recv.at[1], pair, me),
    ]

    def first(plane):
        return jnp.where(plane % 2 == 0, by_x, by_y)

    def second(plane):
        return jnp.where(plane % 2 == 0, by_y, by_x)

    def w_copy(kind, hop, plane, owner, peer, from_input=False):
        span_ = pl.ds(owner * shard, shard)
        src = (q_in, o_in)[kind].at[0] if from_input else wbuf.at[kind, span_]
        return remote(
            src, wbuf.at[kind, span_], w_send.at[kind, hop, plane], w_recv.at[kind, owner], sec, peer
        )

    @pl.when(jnp.logical_not(decoding))
    def _():
        for copy in kv:
            copy.start()

    @pl.when(decoding)
    def _():
        for kind in range(2):
            def to_planes(dz, carry):
                w_copy(kind, 0, dz, me, lax.rem(a + dz, planes) * PLANE + j, True).start()
                return carry

            lax.fori_loop(1, planes, to_planes, 0)
            w_copy(kind, 1, 0, me, a * PLANE + first(a), True).start()
            w_copy(kind, 2, 0, me, a * PLANE + second(a), True).start()

    eye = lax.broadcasted_iota(jnp.int32, (tok, tok), 0) == lax.broadcasted_iota(
        jnp.int32, (tok, tok), 1
    )
    earlier = lax.broadcasted_iota(jnp.int32, (tok, tok), 1) < lax.broadcasted_iota(
        jnp.int32, (tok, tok), 0
    )
    lane = lax.broadcasted_iota(jnp.int32, (tok, LANES), 1).astype(F32)
    route_row = routes[...].astype(F32)
    route_col = jnp.sum(jnp.where(eye, route_row, 0.0), axis=1, keepdims=True)
    gate_col = jnp.sum(jnp.where(eye, gates[...], 0.0), axis=1, keepdims=True)
    onehot = jnp.where(lane == route_col, 1.0, 0.0)
    before = jnp.dot(
        jnp.where(earlier, 1.0, 0.0).astype(BF16), onehot.astype(BF16), preferred_element_type=F32
    )
    lrank = jnp.sum(before * onehot, axis=1, keepdims=True)
    slot_col = route_col * cap + lrank
    slot_row = jnp.sum(jnp.where(eye, slot_col, 0.0), axis=0, keepdims=True)
    cnt[me] = jnp.broadcast_to(jnp.sum(onehot, axis=0, keepdims=True), (8, LANES))

    def cnt_copy(k):
        peer = lax.rem(me + k, experts)
        return remote(cnt.at[me], cnt.at[me], cnt_send.at[k], cnt_recv.at[me], sec, peer)

    def cnt_start(k, carry):
        cnt_copy(k).start()
        return carry

    lax.fori_loop(1, experts, cnt_start, 0)

    @pl.when(jnp.logical_not(decoding))
    def _():
        to_mixed.wait()
        pl.semaphore_wait(turn, 1)

    @pl.when(decoding)
    def _():
        def from_planes(kind):
            def body(dz, carry):
                plane = lax.rem(a - dz + planes, planes)
                owner = plane * PLANE + j
                w_copy(kind, 0, dz, owner, owner).wait_recv()
                w_copy(kind, 1, dz, owner, a * PLANE + first(plane)).start()
                w_copy(kind, 2, dz, owner, a * PLANE + second(plane)).start()
                return carry

            lax.fori_loop(1, planes, body, 0)

        def pass_on(kind):
            def body(dz, carry):
                plane = lax.rem(a - dz + planes, planes)
                owner = plane * PLANE + first(plane)
                w_copy(kind, 1, dz, owner, a * PLANE + first(plane)).wait_recv()
                w_copy(kind, 3, dz, owner, a * PLANE + second(plane)).start()
                return carry

            lax.fori_loop(0, planes, body, 0)

        def arrive(kind):
            def body(dz, carry):
                plane = lax.rem(a - dz + planes, planes)
                for hop, jj in ((2, second(plane)), (3, 3 - j)):
                    w_copy(kind, hop, dz, plane * PLANE + jj, a * PLANE + second(plane)).wait_recv()
                return carry

            lax.fori_loop(0, planes, body, 0)

        from_planes(0)
        pass_on(0)
        from_planes(1)
        pl.semaphore_signal(turn, inc=1, device_id=(pair, me), device_id_type=MESH)
        pass_on(1)
        to_vmem.wait()
        own[0].wait()
        arrive(0)
        tile = 256

        @pl.loop(0, width // tile)
        def _(n):
            cols = pl.ds(pl.multiple_of(n * tile, tile), tile)
            qbuf[:, cols] = jnp.dot(
                tok_vmem[...], wbuf[0, :, cols], preferred_element_type=F32
            ).astype(BF16)

        own[2].wait()
        own[3].wait()
        for copy in kv:
            copy.wait_recv()
        head_dim = width // HEADS
        length = lengths[0, 0]
        valid = lax.broadcasted_iota(jnp.int32, (tok, 2 * span), 1) < length
        low = lax.broadcasted_iota(jnp.int32, (tok, 2 * head_dim), 1) < head_dim
        mask_low = jnp.where(low, 1.0, 0.0).astype(BF16)
        mask_high = jnp.where(low, 0.0, 1.0).astype(BF16)
        scale = 1.0 / (head_dim ** 0.5)

        @pl.loop(0, HEADS // 2)
        def _(i):
            cols = pl.ds(pl.multiple_of(i * 2 * head_dim, 2 * head_dim), 2 * head_dim)
            q2, k2, v2 = qbuf[:, cols], kbuf[:, cols], vbuf[:, cols]
            parts = []
            for mask in (mask_low, mask_high):
                scores = lax.dot_general(
                    q2 * mask, k2, (((1,), (1,)), ((), ())), preferred_element_type=F32
                ) * scale
                scores = jnp.where(valid, scores, -1e30)
                scores = scores - jnp.max(scores, axis=-1, keepdims=True)
                weights = jnp.exp(scores)
                probs = (weights / jnp.sum(weights, axis=-1, keepdims=True)).astype(BF16)
                parts.append(jnp.dot(probs, v2, preferred_element_type=F32))
            cbuf[:, cols] = jnp.where(low, parts[0], parts[1]).astype(BF16)

        own[1].wait()
        arrive(1)

        @pl.loop(0, width // tile)
        def _(n):
            cols = pl.ds(pl.multiple_of(n * tile, tile), tile)
            attn = jnp.dot(cbuf[...], wbuf[1, :, cols], preferred_element_type=F32)
            mixed[:, cols] = (tok_vmem[:, cols].astype(F32) + attn).astype(BF16)

    def block(index):
        return pl.ds(pl.multiple_of(index * cap, cap), cap)

    def fwd_copy(peer):
        return remote(
            buf.at[block(peer)], recv.at[block(me)], fwd_send.at[peer], fwd_recv.at[me], sec, peer
        )

    def fwd_arrival(src):
        return remote(
            buf.at[block(src)], recv.at[block(src)], fwd_send.at[src], fwd_recv.at[src], sec, src
        )

    def ret_copy(peer):
        return remote(
            acts.at[block(peer)], back.at[block(me)], ret_send.at[peer], ret_recv.at[me], sec, peer
        )

    def ret_arrival(src):
        return remote(
            acts.at[block(src)], back.at[block(src)], ret_send.at[src], ret_recv.at[src], sec, src
        )

    def in_plane(plane, visit):
        for s in range(PLANE):
            peer = plane * PLANE + lax.rem(j + s, PLANE)
            if s > 0:
                visit(peer)
            else:
                @pl.when(plane != a)
                def _():
                    visit(peer)

    def group(plane):
        return pl.ds(pl.multiple_of(plane * rows, rows), rows)

    def dispatch(dz, carry):
        plane = lax.rem(a + dz, planes)
        at = (lax.broadcasted_iota(jnp.int32, (rows, tok), 0) + plane * rows).astype(F32)
        placing = jnp.where(slot_row == at, 1.0, 0.0).astype(BF16)
        buf[group(plane), :] = jnp.dot(placing, mixed[...], preferred_element_type=F32).astype(BF16)
        in_plane(plane, lambda peer: fwd_copy(peer).start())
        return carry

    lax.fori_loop(0, planes, dispatch, 0)
    recv[block(me), :] = buf[block(me), :]

    def cnt_wait(k, carry):
        src = lax.rem(me + k, experts)
        remote(cnt.at[src], cnt.at[src], cnt_send.at[k], cnt_recv.at[src], sec, src).wait_recv()
        return carry

    lax.fori_loop(1, experts, cnt_wait, 0)
    get_w.wait()
    counts = cnt[:, 0, :].astype(BF16)
    limit = capacity[0, 0].astype(F32)

    def expert(dz, carry):
        plane = lax.rem(a - dz + planes, planes)
        in_plane(plane, lambda src: fwd_arrival(src).wait_recv())
        act = jnp.maximum(
            jnp.dot(recv[group(plane), :], w_vmem[...], preferred_element_type=F32), 0.0
        )
        row = lax.broadcasted_iota(jnp.int32, (rows, experts), 0)
        source = lax.broadcasted_iota(jnp.int32, (rows, experts), 1)
        lower = jnp.where(source < plane * PLANE + row // cap, 1.0, 0.0).astype(BF16)
        sums = jnp.dot(lower, counts, preferred_element_type=F32)
        mine = lax.broadcasted_iota(jnp.int32, (rows, LANES), 1) == me
        offset = jnp.sum(jnp.where(mine, sums, 0.0), axis=1, keepdims=True)
        rank = offset + (lax.broadcasted_iota(jnp.int32, (rows, 1), 0) % cap).astype(F32)
        kept = jnp.where(rank < limit, 1.0, 0.0)
        acts[group(plane), :] = (act * kept).astype(BF16)
        in_plane(plane, lambda peer: ret_copy(peer).start())
        return carry

    lax.fori_loop(0, planes, expert, 0)
    back[block(me), :] = acts[block(me), :]
    acc[...] = jnp.zeros_like(acc)

    def combine(dz, carry):
        plane = lax.rem(a - dz + planes, planes)
        in_plane(plane, lambda src: ret_arrival(src).wait_recv())
        at = (lax.broadcasted_iota(jnp.int32, (tok, rows), 1) + plane * rows).astype(F32)
        placing = jnp.where(slot_col == at, 1.0, 0.0).astype(BF16)
        acc[...] += jnp.dot(placing, back[group(plane), :], preferred_element_type=F32)
        return carry

    lax.fori_loop(0, planes, combine, 0)
    out[0] = (acc[...] * gate_col).astype(BF16)

    def sent(k, carry):
        peer = lax.rem(me + k, experts)
        cnt_copy(k).wait_send()
        fwd_copy(peer).wait_send()
        ret_copy(peer).wait_send()
        return carry

    lax.fori_loop(1, experts, sent, 0)

    @pl.when(jnp.logical_not(decoding))
    def _():
        for copy in kv:
            copy.wait_send()

    @pl.when(decoding)
    def _():
        for kind in range(2):
            def w_sent(dz, carry):
                for hop in range(4):
                    def done():
                        w_copy(kind, hop, dz, me, a * PLANE + by_x).wait_send()

                    if hop == 0:
                        pl.when(dz > 0)(done)
                    else:
                        done()
                return carry

            lax.fori_loop(0, planes, w_sent, 0)


def shards(
    tokens, gates, routes, capacity, mem_lengths, mem_keys, mem_values, q_weight, out_weight, w_in
):
    sections = lax.axis_size("section")
    experts = lax.axis_size("expert")
    tok, width = tokens.shape[1:]
    hidden = w_in.shape[3]
    span = mem_keys.shape[1]
    cap = max(16, 2 * tok // experts)
    slots = experts * cap
    planes = experts // PLANE
    dma = pltpu.SemaphoreType.DMA
    vmem = pl.BlockSpec(memory_space=pltpu.VMEM)
    smem = pl.BlockSpec(memory_space=pltpu.SMEM)
    hbm = pl.BlockSpec(memory_space=pl.ANY)
    return pl.pallas_call(
        functools.partial(relay, sections, experts, cap),
        out_shape=jax.ShapeDtypeStruct((1, tok, hidden), BF16),
        in_specs=[hbm, vmem, vmem, smem, smem, hbm, hbm, hbm, hbm, hbm],
        out_specs=vmem,
        scratch_shapes=[
            pltpu.VMEM((width, hidden), BF16),
            pltpu.VMEM((tok, width), BF16),
            pltpu.VMEM((2, width, width), BF16),
            pltpu.VMEM((2 * span, width), BF16),
            pltpu.VMEM((2 * span, width), BF16),
            pltpu.VMEM((tok, width), BF16),
            pltpu.VMEM((tok, width), BF16),
            pltpu.VMEM((tok, width), BF16),
            pltpu.VMEM((slots, width), BF16),
            pltpu.VMEM((slots, width), BF16),
            pltpu.VMEM((slots, hidden), BF16),
            pltpu.VMEM((slots, hidden), BF16),
            pltpu.VMEM((tok, hidden), F32),
            pltpu.VMEM((experts, 8, LANES), F32),
            pltpu.SemaphoreType.REGULAR,
            dma((6,)),
            dma((2,)),
            dma((2,)),
            dma((2, 4, planes)),
            dma((2, experts)),
            dma((experts,)),
            dma((experts,)),
            dma((experts,)),
            dma((experts,)),
            dma((experts,)),
            dma((experts,)),
        ],
        compiler_params=pltpu.CompilerParams(
            collective_id=0, has_side_effects=True, vmem_limit_bytes=63 * 1024 * 1024
        ),
        cost_estimate=pl.CostEstimate(
            flops=4 * tok * width * width + 2 * slots * width * hidden,
            bytes_accessed=2 * width * hidden + 8 * width * width,
            transcendentals=HEADS * tok * 2 * span,
        ),
    )(
        tokens, gates, routes.reshape(1, tok), capacity, mem_lengths,
        mem_keys, mem_values, q_weight, out_weight, w_in,
    )


def solution(mesh):
    in_specs = (
        P("section", "expert", None),
        P("section", "expert"),
        P("section", "expert", None),
        P("section", "expert"),
        P("section", "expert"),
        P("section", "expert", None),
        P("section", "expert", None),
        P("section", "expert", None),
        P("section", "expert", None),
        P("section", "expert", None, None),
    )
    out_specs = P("section", "expert", None)
    return jax.shard_map(shards, mesh=mesh, in_specs=in_specs, out_specs=out_specs, check_vma=False)
```

```python
import functools

import jax
import jax.numpy as jnp
from jax import lax
from jax.experimental import pallas as pl
from jax.experimental.pallas import tpu as pltpu
from jax.sharding import PartitionSpec as P

HEADS = 16
LANES = 128
PLANE = 4
MESH = pl.DeviceIdType.MESH
F32 = jnp.float32
BF16 = jnp.bfloat16


def relay(
    sections, experts, cap,
    tokens, gates, routes, capacity, lengths, mem_k, mem_v, q_in, o_in, w_hbm,
    out,
    w_vmem, tok_vmem, wbuf, kbuf, vbuf, qbuf, cbuf, mixed, buf, recv, acts, back, acc, cnt,
    turn, local_sem, kv_send, kv_recv, w_send, w_recv,
    cnt_send, cnt_recv, fwd_send, fwd_recv, ret_send, ret_recv,
):
    half = sections // 2
    planes = experts // PLANE
    tok = tokens.shape[1]
    width = tokens.shape[2]
    span = mem_k.shape[1]
    shard = q_in.shape[1]
    rows = PLANE * cap
    sec = lax.axis_index("section")
    me = lax.axis_index("expert")
    a, j = me // PLANE, me % PLANE
    jy, jx = j // 2, j % 2
    by_x = jy * 2 + (1 - jx)
    by_y = (1 - jy) * 2 + jx
    decoding = sec >= half
    pair = lax.rem(sec + half, sections)

    def remote(src, dst, send, recv_sem, section, peer):
        return pltpu.make_async_remote_copy(
            src_ref=src, dst_ref=dst, send_sem=send, recv_sem=recv_sem,
            device_id=(section, peer), device_id_type=MESH,
        )

    get_w = pltpu.make_async_copy(w_hbm.at[0, 0], w_vmem, local_sem.at[0])
    get_w.start()
    to_mixed = pltpu.make_async_copy(tokens.at[0], mixed, local_sem.at[5])
    to_vmem = pltpu.make_async_copy(tokens.at[0], tok_vmem, local_sem.at[5])
    own_rows = pl.ds(me * shard, shard)
    own = [
        pltpu.make_async_copy(q_in.at[0], wbuf.at[0, own_rows], local_sem.at[1]),
        pltpu.make_async_copy(o_in.at[0], wbuf.at[1, own_rows], local_sem.at[2]),
        pltpu.make_async_copy(mem_k.at[0], kbuf.at[pl.ds(span, span)], local_sem.at[3]),
        pltpu.make_async_copy(mem_v.at[0], vbuf.at[pl.ds(span, span)], local_sem.at[4]),
    ]

    @pl.when(jnp.logical_not(decoding))
    def _():
        to_mixed.start()

    @pl.when(decoding)
    def _():
        to_vmem.start()
        for copy in own:
            copy.start()

    barrier = pltpu.get_barrier_semaphore()

    def greet(k, carry):
        pl.semaphore_signal(
            barrier, inc=1, device_id=(sec, lax.rem(me + k, experts)), device_id_type=MESH
        )
        return carry

    lax.fori_loop(1, experts, greet, 0)
    pl.semaphore_signal(barrier, inc=1, device_id=(pair, me), device_id_type=MESH)
    pl.semaphore_wait(barrier, experts)

    kv = [
        remote(mem_k.at[0], kbuf.at[pl.ds(0, span)], kv_send.at[0], kv_recv.at[0], pair, me),
        remote(mem_v.at[0], vbuf.at[pl.ds(0, span)], kv_send.at[1], kv_recv.at[1], pair, me),
    ]

    def first(plane):
        return jnp.where(plane % 2 == 0, by_x, by_y)

    def second(plane):
        return jnp.where(plane % 2 == 0, by_y, by_x)

    def w_copy(kind, hop, plane, owner, peer, from_input=False):
        span_ = pl.ds(owner * shard, shard)
        src = (q_in, o_in)[kind].at[0] if from_input else wbuf.at[kind, span_]
        return remote(
            src, wbuf.at[kind, span_], w_send.at[kind, hop, plane], w_recv.at[kind, owner], sec, peer
        )

    @pl.when(jnp.logical_not(decoding))
    def _():
        for copy in kv:
            copy.start()

    @pl.when(decoding)
    def _():
        for kind in range(2):
            def to_planes(dz, carry):
                w_copy(kind, 0, dz, me, lax.rem(a + dz, planes) * PLANE + j, True).start()
                return carry

            lax.fori_loop(1, planes, to_planes, 0)
            w_copy(kind, 1, 0, me, a * PLANE + first(a), True).start()
            w_copy(kind, 2, 0, me, a * PLANE + second(a), True).start()

    eye = lax.broadcasted_iota(jnp.int32, (tok, tok), 0) == lax.broadcasted_iota(
        jnp.int32, (tok, tok), 1
    )
    earlier = lax.broadcasted_iota(jnp.int32, (tok, tok), 1) < lax.broadcasted_iota(
        jnp.int32, (tok, tok), 0
    )
    lane = lax.broadcasted_iota(jnp.int32, (tok, LANES), 1).astype(F32)
    route_row = routes[...].astype(F32)
    route_col = jnp.sum(jnp.where(eye, route_row, 0.0), axis=1, keepdims=True)
    gate_col = jnp.sum(jnp.where(eye, gates[...], 0.0), axis=1, keepdims=True)
    onehot = jnp.where(lane == route_col, 1.0, 0.0)
    before = jnp.dot(
        jnp.where(earlier, 1.0, 0.0).astype(BF16), onehot.astype(BF16), preferred_element_type=F32
    )
    lrank = jnp.sum(before * onehot, axis=1, keepdims=True)
    slot_col = route_col * cap + lrank
    slot_row = jnp.sum(jnp.where(eye, slot_col, 0.0), axis=0, keepdims=True)
    cnt[me] = jnp.broadcast_to(jnp.sum(onehot, axis=0, keepdims=True), (8, LANES))

    def cnt_copy(k):
        peer = lax.rem(me + k, experts)
        return remote(cnt.at[me], cnt.at[me], cnt_send.at[k], cnt_recv.at[me], sec, peer)

    def cnt_start(k, carry):
        cnt_copy(k).start()
        return carry

    lax.fori_loop(1, experts, cnt_start, 0)

    @pl.when(jnp.logical_not(decoding))
    def _():
        to_mixed.wait()
        pl.semaphore_wait(turn, 1)

    @pl.when(decoding)
    def _():
        def from_planes(kind):
            def body(dz, carry):
                plane = lax.rem(a - dz + planes, planes)
                owner = plane * PLANE + j
                w_copy(kind, 0, dz, owner, owner).wait_recv()
                w_copy(kind, 1, dz, owner, a * PLANE + first(plane)).start()
                w_copy(kind, 2, dz, owner, a * PLANE + second(plane)).start()
                return carry

            lax.fori_loop(1, planes, body, 0)

        def pass_on(kind):
            def body(dz, carry):
                plane = lax.rem(a - dz + planes, planes)
                owner = plane * PLANE + first(plane)
                w_copy(kind, 1, dz, owner, a * PLANE + first(plane)).wait_recv()
                w_copy(kind, 3, dz, owner, a * PLANE + second(plane)).start()
                return carry

            lax.fori_loop(0, planes, body, 0)

        def arrive(kind):
            def body(dz, carry):
                plane = lax.rem(a - dz + planes, planes)
                for hop, jj in ((2, second(plane)), (3, 3 - j)):
                    w_copy(kind, hop, dz, plane * PLANE + jj, a * PLANE + second(plane)).wait_recv()
                return carry

            lax.fori_loop(0, planes, body, 0)

        from_planes(0)
        pass_on(0)
        from_planes(1)
        pl.semaphore_signal(turn, inc=1, device_id=(pair, me), device_id_type=MESH)
        pass_on(1)
        to_vmem.wait()
        own[0].wait()
        arrive(0)
        tile = 256

        @pl.loop(0, width // tile)
        def _(n):
            cols = pl.ds(pl.multiple_of(n * tile, tile), tile)
            qbuf[:, cols] = jnp.dot(
                tok_vmem[...], wbuf[0, :, cols], preferred_element_type=F32
            ).astype(BF16)

        own[2].wait()
        own[3].wait()
        for copy in kv:
            copy.wait_recv()
        head_dim = width // HEADS
        length = lengths[0, 0]
        valid = lax.broadcasted_iota(jnp.int32, (tok, 2 * span), 1) < length
        low = lax.broadcasted_iota(jnp.int32, (tok, 2 * head_dim), 1) < head_dim
        mask_low = jnp.where(low, 1.0, 0.0).astype(BF16)
        mask_high = jnp.where(low, 0.0, 1.0).astype(BF16)
        scale = 1.0 / (head_dim ** 0.5)

        @pl.loop(0, HEADS // 2)
        def _(i):
            cols = pl.ds(pl.multiple_of(i * 2 * head_dim, 2 * head_dim), 2 * head_dim)
            q2, k2, v2 = qbuf[:, cols], kbuf[:, cols], vbuf[:, cols]
            parts = []
            for mask in (mask_low, mask_high):
                scores = lax.dot_general(
                    q2 * mask, k2, (((1,), (1,)), ((), ())), preferred_element_type=F32
                ) * scale
                scores = jnp.where(valid, scores, -1e30)
                scores = scores - jnp.max(scores, axis=-1, keepdims=True)
                weights = jnp.exp(scores)
                probs = (weights / jnp.sum(weights, axis=-1, keepdims=True)).astype(BF16)
                parts.append(jnp.dot(probs, v2, preferred_element_type=F32))
            cbuf[:, cols] = jnp.where(low, parts[0], parts[1]).astype(BF16)

        own[1].wait()
        arrive(1)

        @pl.loop(0, width // tile)
        def _(n):
            cols = pl.ds(pl.multiple_of(n * tile, tile), tile)
            attn = jnp.dot(cbuf[...], wbuf[1, :, cols], preferred_element_type=F32)
            mixed[:, cols] = (tok_vmem[:, cols].astype(F32) + attn).astype(BF16)

    def block(index):
        return pl.ds(pl.multiple_of(index * cap, cap), cap)

    def fwd_copy(peer):
        return remote(
            buf.at[block(peer)], recv.at[block(me)], fwd_send.at[peer], fwd_recv.at[me], sec, peer
        )

    def fwd_arrival(src):
        return remote(
            buf.at[block(src)], recv.at[block(src)], fwd_send.at[src], fwd_recv.at[src], sec, src
        )

    def ret_copy(peer):
        return remote(
            acts.at[block(peer)], back.at[block(me)], ret_send.at[peer], ret_recv.at[me], sec, peer
        )

    def ret_arrival(src):
        return remote(
            acts.at[block(src)], back.at[block(src)], ret_send.at[src], ret_recv.at[src], sec, src
        )

    def in_plane(plane, visit):
        for s in range(PLANE):
            peer = plane * PLANE + lax.rem(j + s, PLANE)
            if s > 0:
                visit(peer)
            else:
                @pl.when(plane != a)
                def _():
                    visit(peer)

    mid = max(planes // 2, 1)
    side = a // mid

    def visit_order(t):
        across = jnp.where(t < planes - mid, 1, 0)
        base = lax.rem(side + across, planes // mid) * mid
        return base + lax.rem(a + t + 1 - across, mid)

    def group(plane):
        return pl.ds(pl.multiple_of(plane * rows, rows), rows)

    def dispatch(dz, carry):
        plane = visit_order(dz)
        at = (lax.broadcasted_iota(jnp.int32, (rows, tok), 0) + plane * rows).astype(F32)
        placing = jnp.where(slot_row == at, 1.0, 0.0).astype(BF16)
        buf[group(plane), :] = jnp.dot(placing, mixed[...], preferred_element_type=F32).astype(BF16)
        in_plane(plane, lambda peer: fwd_copy(peer).start())
        return carry

    lax.fori_loop(0, planes, dispatch, 0)
    recv[block(me), :] = buf[block(me), :]

    def cnt_wait(k, carry):
        src = lax.rem(me + k, experts)
        remote(cnt.at[src], cnt.at[src], cnt_send.at[k], cnt_recv.at[src], sec, src).wait_recv()
        return carry

    lax.fori_loop(1, experts, cnt_wait, 0)
    get_w.wait()
    counts = cnt[:, 0, :].astype(BF16)
    limit = capacity[0, 0].astype(F32)

    def expert(dz, carry):
        plane = visit_order(dz)
        in_plane(plane, lambda src: fwd_arrival(src).wait_recv())
        act = jnp.maximum(
            jnp.dot(recv[group(plane), :], w_vmem[...], preferred_element_type=F32), 0.0
        )
        row = lax.broadcasted_iota(jnp.int32, (rows, experts), 0)
        source = lax.broadcasted_iota(jnp.int32, (rows, experts), 1)
        lower = jnp.where(source < plane * PLANE + row // cap, 1.0, 0.0).astype(BF16)
        sums = jnp.dot(lower, counts, preferred_element_type=F32)
        mine = lax.broadcasted_iota(jnp.int32, (rows, LANES), 1) == me
        offset = jnp.sum(jnp.where(mine, sums, 0.0), axis=1, keepdims=True)
        rank = offset + (lax.broadcasted_iota(jnp.int32, (rows, 1), 0) % cap).astype(F32)
        kept = jnp.where(rank < limit, 1.0, 0.0)
        acts[group(plane), :] = (act * kept).astype(BF16)
        in_plane(plane, lambda peer: ret_copy(peer).start())
        return carry

    lax.fori_loop(0, planes, expert, 0)
    back[block(me), :] = acts[block(me), :]
    acc[...] = jnp.zeros_like(acc)

    def combine(dz, carry):
        plane = visit_order(dz)
        in_plane(plane, lambda src: ret_arrival(src).wait_recv())
        at = (lax.broadcasted_iota(jnp.int32, (tok, rows), 1) + plane * rows).astype(F32)
        placing = jnp.where(slot_col == at, 1.0, 0.0).astype(BF16)
        acc[...] += jnp.dot(placing, back[group(plane), :], preferred_element_type=F32)
        return carry

    lax.fori_loop(0, planes, combine, 0)
    out[0] = (acc[...] * gate_col).astype(BF16)

    def sent(k, carry):
        peer = lax.rem(me + k, experts)
        cnt_copy(k).wait_send()
        fwd_copy(peer).wait_send()
        ret_copy(peer).wait_send()
        return carry

    lax.fori_loop(1, experts, sent, 0)

    @pl.when(jnp.logical_not(decoding))
    def _():
        for copy in kv:
            copy.wait_send()

    @pl.when(decoding)
    def _():
        for kind in range(2):
            def w_sent(dz, carry):
                for hop in range(4):
                    def done():
                        w_copy(kind, hop, dz, me, a * PLANE + by_x).wait_send()

                    if hop == 0:
                        pl.when(dz > 0)(done)
                    else:
                        done()
                return carry

            lax.fori_loop(0, planes, w_sent, 0)


def shards(
    tokens, gates, routes, capacity, mem_lengths, mem_keys, mem_values, q_weight, out_weight, w_in
):
    sections = lax.axis_size("section")
    experts = lax.axis_size("expert")
    tok, width = tokens.shape[1:]
    hidden = w_in.shape[3]
    span = mem_keys.shape[1]
    cap = max(16, 2 * tok // experts)
    slots = experts * cap
    planes = experts // PLANE
    dma = pltpu.SemaphoreType.DMA
    vmem = pl.BlockSpec(memory_space=pltpu.VMEM)
    smem = pl.BlockSpec(memory_space=pltpu.SMEM)
    hbm = pl.BlockSpec(memory_space=pl.ANY)
    return pl.pallas_call(
        functools.partial(relay, sections, experts, cap),
        out_shape=jax.ShapeDtypeStruct((1, tok, hidden), BF16),
        in_specs=[hbm, vmem, vmem, smem, smem, hbm, hbm, hbm, hbm, hbm],
        out_specs=vmem,
        scratch_shapes=[
            pltpu.VMEM((width, hidden), BF16),
            pltpu.VMEM((tok, width), BF16),
            pltpu.VMEM((2, width, width), BF16),
            pltpu.VMEM((2 * span, width), BF16),
            pltpu.VMEM((2 * span, width), BF16),
            pltpu.VMEM((tok, width), BF16),
            pltpu.VMEM((tok, width), BF16),
            pltpu.VMEM((tok, width), BF16),
            pltpu.VMEM((slots, width), BF16),
            pltpu.VMEM((slots, width), BF16),
            pltpu.VMEM((slots, hidden), BF16),
            pltpu.VMEM((slots, hidden), BF16),
            pltpu.VMEM((tok, hidden), F32),
            pltpu.VMEM((experts, 8, LANES), F32),
            pltpu.SemaphoreType.REGULAR,
            dma((6,)),
            dma((2,)),
            dma((2,)),
            dma((2, 4, planes)),
            dma((2, experts)),
            dma((experts,)),
            dma((experts,)),
            dma((experts,)),
            dma((experts,)),
            dma((experts,)),
            dma((experts,)),
        ],
        compiler_params=pltpu.CompilerParams(
            collective_id=0, has_side_effects=True, vmem_limit_bytes=63 * 1024 * 1024
        ),
        cost_estimate=pl.CostEstimate(
            flops=4 * tok * width * width + 2 * slots * width * hidden,
            bytes_accessed=2 * width * hidden + 8 * width * width,
            transcendentals=HEADS * tok * 2 * span,
        ),
    )(
        tokens, gates, routes.reshape(1, tok), capacity, mem_lengths,
        mem_keys, mem_values, q_weight, out_weight, w_in,
    )


def solution(mesh):
    in_specs = (
        P("section", "expert", None),
        P("section", "expert"),
        P("section", "expert", None),
        P("section", "expert"),
        P("section", "expert"),
        P("section", "expert", None),
        P("section", "expert", None),
        P("section", "expert", None),
        P("section", "expert", None),
        P("section", "expert", None, None),
    )
    out_specs = P("section", "expert", None)
    return jax.shard_map(shards, mesh=mesh, in_specs=in_specs, out_specs=out_specs, check_vma=False)
```

```python
import functools

import jax
import jax.numpy as jnp
from jax import lax
from jax.experimental import pallas as pl
from jax.experimental.pallas import tpu as pltpu
from jax.sharding import PartitionSpec as P

HEADS = 16
LANES = 128
PLANE = 4
MESH = pl.DeviceIdType.MESH
F32 = jnp.float32
BF16 = jnp.bfloat16


def relay(
    sections, experts, cap,
    tokens, gates, routes, capacity, lengths, mem_k, mem_v, q_in, o_in, w_hbm,
    out,
    w_vmem, tok_vmem, wbuf, kbuf, vbuf, qbuf, cbuf, mixed, buf, recv, acts, back, acc, cnt,
    turn, local_sem, kv_send, kv_recv, w_send, w_recv,
    cnt_send, cnt_recv, fwd_send, fwd_recv, ret_send, ret_recv,
):
    half = sections // 2
    planes = experts // PLANE
    tok = tokens.shape[1]
    width = tokens.shape[2]
    span = mem_k.shape[1]
    shard = q_in.shape[1]
    rows = PLANE * cap
    sec = lax.axis_index("section")
    me = lax.axis_index("expert")
    a, j = me // PLANE, me % PLANE
    jy, jx = j // 2, j % 2
    by_x = jy * 2 + (1 - jx)
    by_y = (1 - jy) * 2 + jx
    decoding = sec >= half
    pair = lax.rem(sec + half, sections)

    def remote(src, dst, send, recv_sem, section, peer):
        return pltpu.make_async_remote_copy(
            src_ref=src, dst_ref=dst, send_sem=send, recv_sem=recv_sem,
            device_id=(section, peer), device_id_type=MESH,
        )

    get_w = pltpu.make_async_copy(w_hbm.at[0, 0], w_vmem, local_sem.at[0])
    get_w.start()
    to_mixed = pltpu.make_async_copy(tokens.at[0], mixed, local_sem.at[5])
    to_vmem = pltpu.make_async_copy(tokens.at[0], tok_vmem, local_sem.at[5])
    own_rows = pl.ds(me * shard, shard)
    own = [
        pltpu.make_async_copy(q_in.at[0], wbuf.at[0, own_rows], local_sem.at[1]),
        pltpu.make_async_copy(o_in.at[0], wbuf.at[1, own_rows], local_sem.at[2]),
        pltpu.make_async_copy(mem_k.at[0], kbuf.at[pl.ds(span, span)], local_sem.at[3]),
        pltpu.make_async_copy(mem_v.at[0], vbuf.at[pl.ds(span, span)], local_sem.at[4]),
    ]

    @pl.when(jnp.logical_not(decoding))
    def _():
        to_mixed.start()

    @pl.when(decoding)
    def _():
        to_vmem.start()
        for copy in own:
            copy.start()

    barrier = pltpu.get_barrier_semaphore()

    def greet(k, carry):
        pl.semaphore_signal(
            barrier, inc=1, device_id=(sec, lax.rem(me + k, experts)), device_id_type=MESH
        )
        return carry

    lax.fori_loop(1, experts, greet, 0)
    pl.semaphore_signal(barrier, inc=1, device_id=(pair, me), device_id_type=MESH)
    pl.semaphore_wait(barrier, experts)

    kv = [
        remote(mem_k.at[0], kbuf.at[pl.ds(0, span)], kv_send.at[0], kv_recv.at[0], pair, me),
        remote(mem_v.at[0], vbuf.at[pl.ds(0, span)], kv_send.at[1], kv_recv.at[1], pair, me),
    ]

    def first(plane):
        return jnp.where(plane % 2 == 0, by_x, by_y)

    def second(plane):
        return jnp.where(plane % 2 == 0, by_y, by_x)

    def w_copy(kind, hop, plane, owner, peer, from_input=False):
        span_ = pl.ds(owner * shard, shard)
        src = (q_in, o_in)[kind].at[0] if from_input else wbuf.at[kind, span_]
        return remote(
            src, wbuf.at[kind, span_], w_send.at[kind, hop, plane], w_recv.at[kind, owner], sec, peer
        )

    @pl.when(jnp.logical_not(decoding))
    def _():
        for copy in kv:
            copy.start()

    @pl.when(decoding)
    def _():
        for kind in range(2):
            @pl.when(a + 1 < planes)
            def _():
                w_copy(kind, 0, a, me, me + PLANE, True).start()

            @pl.when(a >= 1)
            def _():
                w_copy(kind, 4, a, me, me - PLANE, True).start()

            w_copy(kind, 1, a, me, a * PLANE + first(a), True).start()
            w_copy(kind, 2, a, me, a * PLANE + second(a), True).start()

    eye = lax.broadcasted_iota(jnp.int32, (tok, tok), 0) == lax.broadcasted_iota(
        jnp.int32, (tok, tok), 1
    )
    earlier = lax.broadcasted_iota(jnp.int32, (tok, tok), 1) < lax.broadcasted_iota(
        jnp.int32, (tok, tok), 0
    )
    lane = lax.broadcasted_iota(jnp.int32, (tok, LANES), 1).astype(F32)
    route_row = routes[...].astype(F32)
    route_col = jnp.sum(jnp.where(eye, route_row, 0.0), axis=1, keepdims=True)
    gate_col = jnp.sum(jnp.where(eye, gates[...], 0.0), axis=1, keepdims=True)
    onehot = jnp.where(lane == route_col, 1.0, 0.0)
    before = jnp.dot(
        jnp.where(earlier, 1.0, 0.0).astype(BF16), onehot.astype(BF16), preferred_element_type=F32
    )
    lrank = jnp.sum(before * onehot, axis=1, keepdims=True)
    slot_col = route_col * cap + lrank
    slot_row = jnp.sum(jnp.where(eye, slot_col, 0.0), axis=0, keepdims=True)
    cnt[me] = jnp.broadcast_to(jnp.sum(onehot, axis=0, keepdims=True), (8, LANES))

    def cnt_copy(k):
        peer = lax.rem(me + k, experts)
        return remote(cnt.at[me], cnt.at[me], cnt_send.at[k], cnt_recv.at[me], sec, peer)

    def cnt_start(k, carry):
        cnt_copy(k).start()
        return carry

    lax.fori_loop(1, experts, cnt_start, 0)

    @pl.when(jnp.logical_not(decoding))
    def _():
        to_mixed.wait()
        pl.semaphore_wait(turn, 1)

    @pl.when(decoding)
    def _():
        def nearest(visit):
            def body(dz, carry):
                for step in (-1, 1):
                    plane = a + step * dz

                    @pl.when(jnp.logical_and(plane >= 0, plane < planes))
                    def _():
                        visit(plane, a - step)

                return carry

            lax.fori_loop(1, planes, body, 0)

        def from_planes(kind):
            def visit(plane, onward):
                owner = plane * PLANE + j
                w_copy(kind, 0, plane, owner, owner).wait_recv()

                @pl.when(jnp.logical_and(onward >= 0, onward < planes))
                def _():
                    w_copy(kind, 0, plane, owner, onward * PLANE + j).start()

                w_copy(kind, 1, plane, owner, a * PLANE + first(plane)).start()
                w_copy(kind, 2, plane, owner, a * PLANE + second(plane)).start()

            nearest(visit)

        def pass_on(kind):
            def visit(plane, onward):
                owner = plane * PLANE + first(plane)
                w_copy(kind, 1, plane, owner, a * PLANE + first(plane)).wait_recv()
                w_copy(kind, 3, plane, owner, a * PLANE + second(plane)).start()

            visit(a, a)
            nearest(visit)

        def arrive(kind):
            def body(dz, carry):
                plane = lax.rem(a - dz + planes, planes)
                for hop, jj in ((2, second(plane)), (3, 3 - j)):
                    w_copy(kind, hop, dz, plane * PLANE + jj, a * PLANE + second(plane)).wait_recv()
                return carry

            lax.fori_loop(0, planes, body, 0)

        from_planes(0)
        pass_on(0)
        from_planes(1)
        pl.semaphore_signal(turn, inc=1, device_id=(pair, me), device_id_type=MESH)
        pass_on(1)
        to_vmem.wait()
        own[0].wait()
        arrive(0)
        tile = 256

        @pl.loop(0, width // tile)
        def _(n):
            cols = pl.ds(pl.multiple_of(n * tile, tile), tile)
            qbuf[:, cols] = jnp.dot(
                tok_vmem[...], wbuf[0, :, cols], preferred_element_type=F32
            ).astype(BF16)

        own[2].wait()
        own[3].wait()
        for copy in kv:
            copy.wait_recv()
        head_dim = width // HEADS
        length = lengths[0, 0]
        valid = lax.broadcasted_iota(jnp.int32, (tok, 2 * span), 1) < length
        low = lax.broadcasted_iota(jnp.int32, (tok, 2 * head_dim), 1) < head_dim
        mask_low = jnp.where(low, 1.0, 0.0).astype(BF16)
        mask_high = jnp.where(low, 0.0, 1.0).astype(BF16)
        scale = 1.0 / (head_dim ** 0.5)

        @pl.loop(0, HEADS // 2)
        def _(i):
            cols = pl.ds(pl.multiple_of(i * 2 * head_dim, 2 * head_dim), 2 * head_dim)
            q2, k2, v2 = qbuf[:, cols], kbuf[:, cols], vbuf[:, cols]
            parts = []
            for mask in (mask_low, mask_high):
                scores = lax.dot_general(
                    q2 * mask, k2, (((1,), (1,)), ((), ())), preferred_element_type=F32
                ) * scale
                scores = jnp.where(valid, scores, -1e30)
                scores = scores - jnp.max(scores, axis=-1, keepdims=True)
                weights = jnp.exp(scores)
                probs = (weights / jnp.sum(weights, axis=-1, keepdims=True)).astype(BF16)
                parts.append(jnp.dot(probs, v2, preferred_element_type=F32))
            cbuf[:, cols] = jnp.where(low, parts[0], parts[1]).astype(BF16)

        own[1].wait()
        arrive(1)

        @pl.loop(0, width // tile)
        def _(n):
            cols = pl.ds(pl.multiple_of(n * tile, tile), tile)
            attn = jnp.dot(cbuf[...], wbuf[1, :, cols], preferred_element_type=F32)
            mixed[:, cols] = (tok_vmem[:, cols].astype(F32) + attn).astype(BF16)

    def block(index):
        return pl.ds(pl.multiple_of(index * cap, cap), cap)

    def fwd_copy(peer):
        return remote(
            buf.at[block(peer)], recv.at[block(me)], fwd_send.at[peer], fwd_recv.at[me], sec, peer
        )

    def fwd_arrival(src):
        return remote(
            buf.at[block(src)], recv.at[block(src)], fwd_send.at[src], fwd_recv.at[src], sec, src
        )

    def ret_copy(peer):
        return remote(
            acts.at[block(peer)], back.at[block(me)], ret_send.at[peer], ret_recv.at[me], sec, peer
        )

    def ret_arrival(src):
        return remote(
            acts.at[block(src)], back.at[block(src)], ret_send.at[src], ret_recv.at[src], sec, src
        )

    def in_plane(plane, visit):
        for s in range(PLANE):
            peer = plane * PLANE + lax.rem(j + s, PLANE)
            if s > 0:
                visit(peer)
            else:
                @pl.when(plane != a)
                def _():
                    visit(peer)

    mid = max(planes // 2, 1)
    side = a // mid

    def visit_order(t):
        across = jnp.where(t < planes - mid, 1, 0)
        base = lax.rem(side + across, planes // mid) * mid
        return base + lax.rem(a + t + 1 - across, mid)

    def group(plane):
        return pl.ds(pl.multiple_of(plane * rows, rows), rows)

    def dispatch(dz, carry):
        plane = visit_order(dz)
        at = (lax.broadcasted_iota(jnp.int32, (rows, tok), 0) + plane * rows).astype(F32)
        placing = jnp.where(slot_row == at, 1.0, 0.0).astype(BF16)
        buf[group(plane), :] = jnp.dot(placing, mixed[...], preferred_element_type=F32).astype(BF16)
        in_plane(plane, lambda peer: fwd_copy(peer).start())
        return carry

    lax.fori_loop(0, planes, dispatch, 0)
    recv[block(me), :] = buf[block(me), :]

    def cnt_wait(k, carry):
        src = lax.rem(me + k, experts)
        remote(cnt.at[src], cnt.at[src], cnt_send.at[k], cnt_recv.at[src], sec, src).wait_recv()
        return carry

    lax.fori_loop(1, experts, cnt_wait, 0)
    get_w.wait()
    counts = cnt[:, 0, :].astype(BF16)
    limit = capacity[0, 0].astype(F32)

    def expert(dz, carry):
        plane = visit_order(dz)
        in_plane(plane, lambda src: fwd_arrival(src).wait_recv())
        act = jnp.maximum(
            jnp.dot(recv[group(plane), :], w_vmem[...], preferred_element_type=F32), 0.0
        )
        row = lax.broadcasted_iota(jnp.int32, (rows, experts), 0)
        source = lax.broadcasted_iota(jnp.int32, (rows, experts), 1)
        lower = jnp.where(source < plane * PLANE + row // cap, 1.0, 0.0).astype(BF16)
        sums = jnp.dot(lower, counts, preferred_element_type=F32)
        mine = lax.broadcasted_iota(jnp.int32, (rows, LANES), 1) == me
        offset = jnp.sum(jnp.where(mine, sums, 0.0), axis=1, keepdims=True)
        rank = offset + (lax.broadcasted_iota(jnp.int32, (rows, 1), 0) % cap).astype(F32)
        kept = jnp.where(rank < limit, 1.0, 0.0)
        acts[group(plane), :] = (act * kept).astype(BF16)
        in_plane(plane, lambda peer: ret_copy(peer).start())
        return carry

    lax.fori_loop(0, planes, expert, 0)
    back[block(me), :] = acts[block(me), :]
    acc[...] = jnp.zeros_like(acc)

    def combine(dz, carry):
        plane = visit_order(dz)
        in_plane(plane, lambda src: ret_arrival(src).wait_recv())
        at = (lax.broadcasted_iota(jnp.int32, (tok, rows), 1) + plane * rows).astype(F32)
        placing = jnp.where(slot_col == at, 1.0, 0.0).astype(BF16)
        acc[...] += jnp.dot(placing, back[group(plane), :], preferred_element_type=F32)
        return carry

    lax.fori_loop(0, planes, combine, 0)
    out[0] = (acc[...] * gate_col).astype(BF16)

    def sent(k, carry):
        peer = lax.rem(me + k, experts)
        cnt_copy(k).wait_send()
        fwd_copy(peer).wait_send()
        ret_copy(peer).wait_send()
        return carry

    lax.fori_loop(1, experts, sent, 0)

    @pl.when(jnp.logical_not(decoding))
    def _():
        for copy in kv:
            copy.wait_send()

    @pl.when(decoding)
    def _():
        for kind in range(2):
            def w_sent(plane, carry):
                def left(hop):
                    w_copy(kind, hop, plane, me, a * PLANE + by_x).wait_send()

                for hop in (1, 2, 3):
                    left(hop)
                upward = plane <= a

                @pl.when(jnp.logical_or(
                    jnp.logical_and(upward, a + 1 < planes),
                    jnp.logical_and(jnp.logical_not(upward), a >= 1),
                ))
                def _():
                    left(0)

                return carry

            lax.fori_loop(0, planes, w_sent, 0)

            @pl.when(a >= 1)
            def _():
                w_copy(kind, 4, a, me, me - PLANE).wait_send()


def shards(
    tokens, gates, routes, capacity, mem_lengths, mem_keys, mem_values, q_weight, out_weight, w_in
):
    sections = lax.axis_size("section")
    experts = lax.axis_size("expert")
    tok, width = tokens.shape[1:]
    hidden = w_in.shape[3]
    span = mem_keys.shape[1]
    cap = max(16, 2 * tok // experts)
    slots = experts * cap
    planes = experts // PLANE
    dma = pltpu.SemaphoreType.DMA
    vmem = pl.BlockSpec(memory_space=pltpu.VMEM)
    smem = pl.BlockSpec(memory_space=pltpu.SMEM)
    hbm = pl.BlockSpec(memory_space=pl.ANY)
    return pl.pallas_call(
        functools.partial(relay, sections, experts, cap),
        out_shape=jax.ShapeDtypeStruct((1, tok, hidden), BF16),
        in_specs=[hbm, vmem, vmem, smem, smem, hbm, hbm, hbm, hbm, hbm],
        out_specs=vmem,
        scratch_shapes=[
            pltpu.VMEM((width, hidden), BF16),
            pltpu.VMEM((tok, width), BF16),
            pltpu.VMEM((2, width, width), BF16),
            pltpu.VMEM((2 * span, width), BF16),
            pltpu.VMEM((2 * span, width), BF16),
            pltpu.VMEM((tok, width), BF16),
            pltpu.VMEM((tok, width), BF16),
            pltpu.VMEM((tok, width), BF16),
            pltpu.VMEM((slots, width), BF16),
            pltpu.VMEM((slots, width), BF16),
            pltpu.VMEM((slots, hidden), BF16),
            pltpu.VMEM((slots, hidden), BF16),
            pltpu.VMEM((tok, hidden), F32),
            pltpu.VMEM((experts, 8, LANES), F32),
            pltpu.SemaphoreType.REGULAR,
            dma((6,)),
            dma((2,)),
            dma((2,)),
            dma((2, 5, planes)),
            dma((2, experts)),
            dma((experts,)),
            dma((experts,)),
            dma((experts,)),
            dma((experts,)),
            dma((experts,)),
            dma((experts,)),
        ],
        compiler_params=pltpu.CompilerParams(
            collective_id=0, has_side_effects=True, vmem_limit_bytes=63 * 1024 * 1024
        ),
        cost_estimate=pl.CostEstimate(
            flops=4 * tok * width * width + 2 * slots * width * hidden,
            bytes_accessed=2 * width * hidden + 8 * width * width,
            transcendentals=HEADS * tok * 2 * span,
        ),
    )(
        tokens, gates, routes.reshape(1, tok), capacity, mem_lengths,
        mem_keys, mem_values, q_weight, out_weight, w_in,
    )


def solution(mesh):
    in_specs = (
        P("section", "expert", None),
        P("section", "expert"),
        P("section", "expert", None),
        P("section", "expert"),
        P("section", "expert"),
        P("section", "expert", None),
        P("section", "expert", None),
        P("section", "expert", None),
        P("section", "expert", None),
        P("section", "expert", None, None),
    )
    out_specs = P("section", "expert", None)
    return jax.shard_map(shards, mesh=mesh, in_specs=in_specs, out_specs=out_specs, check_vma=False)
```

```python
import functools

import jax
import jax.numpy as jnp
from jax import lax
from jax.experimental import pallas as pl
from jax.experimental.pallas import tpu as pltpu
from jax.sharding import PartitionSpec as P

HEADS = 16
LANES = 128
PLANE = 4
MESH = pl.DeviceIdType.MESH
F32 = jnp.float32
BF16 = jnp.bfloat16


def relay(
    sections, experts, cap,
    tokens, gates, routes, capacity, lengths, mem_k, mem_v, q_in, o_in, w_hbm,
    out,
    w_vmem, tok_vmem, wbuf, kbuf, vbuf, qbuf, cbuf, mixed, buf, recv, acts, back, acc, cnt,
    turn, local_sem, kv_send, kv_recv, w_send, w_recv,
    cnt_send, cnt_recv, fwd_send, fwd_recv, ret_send, ret_recv,
):
    half = sections // 2
    planes = experts // PLANE
    tok = tokens.shape[1]
    width = tokens.shape[2]
    span = mem_k.shape[1]
    shard = q_in.shape[1]
    rows = PLANE * cap
    sec = lax.axis_index("section")
    me = lax.axis_index("expert")
    a, j = me // PLANE, me % PLANE
    jy, jx = j // 2, j % 2
    by_x = jy * 2 + (1 - jx)
    by_y = (1 - jy) * 2 + jx
    decoding = sec >= half
    pair = lax.rem(sec + half, sections)

    def remote(src, dst, send, recv_sem, section, peer):
        return pltpu.make_async_remote_copy(
            src_ref=src, dst_ref=dst, send_sem=send, recv_sem=recv_sem,
            device_id=(section, peer), device_id_type=MESH,
        )

    get_w = pltpu.make_async_copy(w_hbm.at[0, 0], w_vmem, local_sem.at[0])
    get_w.start()
    to_mixed = pltpu.make_async_copy(tokens.at[0], mixed, local_sem.at[5])
    to_vmem = pltpu.make_async_copy(tokens.at[0], tok_vmem, local_sem.at[5])
    own_rows = pl.ds(me * shard, shard)
    own = [
        pltpu.make_async_copy(q_in.at[0], wbuf.at[0, own_rows], local_sem.at[1]),
        pltpu.make_async_copy(o_in.at[0], wbuf.at[1, own_rows], local_sem.at[2]),
        pltpu.make_async_copy(mem_k.at[0], kbuf.at[pl.ds(span, span)], local_sem.at[3]),
        pltpu.make_async_copy(mem_v.at[0], vbuf.at[pl.ds(span, span)], local_sem.at[4]),
    ]

    @pl.when(jnp.logical_not(decoding))
    def _():
        to_mixed.start()

    @pl.when(decoding)
    def _():
        to_vmem.start()
        for copy in own:
            copy.start()

    barrier = pltpu.get_barrier_semaphore()

    def greet(k, carry):
        pl.semaphore_signal(
            barrier, inc=1, device_id=(sec, lax.rem(me + k, experts)), device_id_type=MESH
        )
        return carry

    lax.fori_loop(1, experts, greet, 0)
    pl.semaphore_signal(barrier, inc=1, device_id=(pair, me), device_id_type=MESH)
    pl.semaphore_wait(barrier, experts)

    kv = [
        remote(mem_k.at[0], kbuf.at[pl.ds(0, span)], kv_send.at[0], kv_recv.at[0], pair, me),
        remote(mem_v.at[0], vbuf.at[pl.ds(0, span)], kv_send.at[1], kv_recv.at[1], pair, me),
    ]

    def first(plane):
        return jnp.where(plane % 2 == 0, by_x, by_y)

    def second(plane):
        return jnp.where(plane % 2 == 0, by_y, by_x)

    def w_copy(kind, hop, plane, owner, peer, from_input=False):
        span_ = pl.ds(owner * shard, shard)
        src = (q_in, o_in)[kind].at[0] if from_input else wbuf.at[kind, span_]
        return remote(
            src, wbuf.at[kind, span_], w_send.at[kind, hop, plane], w_recv.at[kind, owner], sec, peer
        )

    @pl.when(jnp.logical_not(decoding))
    def _():
        for copy in kv:
            copy.start()

    @pl.when(decoding)
    def _():
        for kind in range(2):
            def to_planes(dz, carry):
                w_copy(kind, 0, dz, me, lax.rem(a + dz, planes) * PLANE + j, True).start()
                return carry

            lax.fori_loop(1, planes, to_planes, 0)
            w_copy(kind, 1, 0, me, a * PLANE + first(a), True).start()
            w_copy(kind, 2, 0, me, a * PLANE + second(a), True).start()

    eye = lax.broadcasted_iota(jnp.int32, (tok, tok), 0) == lax.broadcasted_iota(
        jnp.int32, (tok, tok), 1
    )
    earlier = lax.broadcasted_iota(jnp.int32, (tok, tok), 1) < lax.broadcasted_iota(
        jnp.int32, (tok, tok), 0
    )
    lane = lax.broadcasted_iota(jnp.int32, (tok, LANES), 1).astype(F32)
    route_row = routes[...].astype(F32)
    route_col = jnp.sum(jnp.where(eye, route_row, 0.0), axis=1, keepdims=True)
    gate_col = jnp.sum(jnp.where(eye, gates[...], 0.0), axis=1, keepdims=True)
    onehot = jnp.where(lane == route_col, 1.0, 0.0)
    before = jnp.dot(
        jnp.where(earlier, 1.0, 0.0).astype(BF16), onehot.astype(BF16), preferred_element_type=F32
    )
    lrank = jnp.sum(before * onehot, axis=1, keepdims=True)
    slot_col = route_col * cap + lrank
    slot_row = jnp.sum(jnp.where(eye, slot_col, 0.0), axis=0, keepdims=True)
    cnt[me] = jnp.broadcast_to(jnp.sum(onehot, axis=0, keepdims=True), (8, LANES))

    def cnt_copy(k):
        peer = lax.rem(me + k, experts)
        return remote(cnt.at[me], cnt.at[me], cnt_send.at[k], cnt_recv.at[me], sec, peer)

    def cnt_start(k, carry):
        cnt_copy(k).start()
        return carry

    lax.fori_loop(1, experts, cnt_start, 0)

    @pl.when(jnp.logical_not(decoding))
    def _():
        to_mixed.wait()
        pl.semaphore_wait(turn, 1)

    @pl.when(decoding)
    def _():
        def from_planes(kind):
            def body(dz, carry):
                plane = lax.rem(a - dz + planes, planes)
                owner = plane * PLANE + j
                w_copy(kind, 0, dz, owner, owner).wait_recv()
                w_copy(kind, 1, dz, owner, a * PLANE + first(plane)).start()
                w_copy(kind, 2, dz, owner, a * PLANE + second(plane)).start()
                return carry

            lax.fori_loop(1, planes, body, 0)

        def pass_on(kind):
            def body(dz, carry):
                plane = lax.rem(a - dz + planes, planes)
                owner = plane * PLANE + first(plane)
                w_copy(kind, 1, dz, owner, a * PLANE + first(plane)).wait_recv()
                w_copy(kind, 3, dz, owner, a * PLANE + second(plane)).start()
                return carry

            lax.fori_loop(0, planes, body, 0)

        def arrive(kind):
            def body(dz, carry):
                plane = lax.rem(a - dz + planes, planes)
                for hop, jj in ((2, second(plane)), (3, 3 - j)):
                    w_copy(kind, hop, dz, plane * PLANE + jj, a * PLANE + second(plane)).wait_recv()
                return carry

            lax.fori_loop(0, planes, body, 0)

        from_planes(0)
        pl.semaphore_signal(turn, inc=1, device_id=(pair, me), device_id_type=MESH)
        pass_on(0)
        from_planes(1)
        pass_on(1)
        to_vmem.wait()
        own[0].wait()
        arrive(0)
        tile = 256

        @pl.loop(0, width // tile)
        def _(n):
            cols = pl.ds(pl.multiple_of(n * tile, tile), tile)
            qbuf[:, cols] = jnp.dot(
                tok_vmem[...], wbuf[0, :, cols], preferred_element_type=F32
            ).astype(BF16)

        own[2].wait()
        own[3].wait()
        for copy in kv:
            copy.wait_recv()
        head_dim = width // HEADS
        length = lengths[0, 0]
        valid = lax.broadcasted_iota(jnp.int32, (tok, 2 * span), 1) < length
        low = lax.broadcasted_iota(jnp.int32, (tok, 2 * head_dim), 1) < head_dim
        scale = 1.0 / (head_dim ** 0.5)
        mask_low = jnp.where(low, scale, 0.0).astype(BF16)
        mask_high = jnp.where(low, 0.0, scale).astype(BF16)

        @pl.loop(0, HEADS // 2)
        def _(i):
            cols = pl.ds(pl.multiple_of(i * 2 * head_dim, 2 * head_dim), 2 * head_dim)
            q2, k2, v2 = qbuf[:, cols], kbuf[:, cols], vbuf[:, cols]
            parts = []
            for mask in (mask_low, mask_high):
                scores = lax.dot_general(
                    q2 * mask, k2, (((1,), (1,)), ((), ())), preferred_element_type=F32
                )
                scores = jnp.where(valid, scores, -1e30)
                scores = scores - jnp.max(scores, axis=-1, keepdims=True)
                weights = jnp.exp(scores)
                probs = (weights * (1.0 / jnp.sum(weights, axis=-1, keepdims=True))).astype(BF16)
                parts.append(jnp.dot(probs, v2, preferred_element_type=F32))
            cbuf[:, cols] = jnp.where(low, parts[0], parts[1]).astype(BF16)

        own[1].wait()
        arrive(1)

        @pl.loop(0, width // tile)
        def _(n):
            cols = pl.ds(pl.multiple_of(n * tile, tile), tile)
            attn = jnp.dot(cbuf[...], wbuf[1, :, cols], preferred_element_type=F32)
            mixed[:, cols] = (tok_vmem[:, cols].astype(F32) + attn).astype(BF16)

    def block(index):
        return pl.ds(pl.multiple_of(index * cap, cap), cap)

    def fwd_copy(peer):
        return remote(
            buf.at[block(peer)], recv.at[block(me)], fwd_send.at[peer], fwd_recv.at[me], sec, peer
        )

    def fwd_arrival(src):
        return remote(
            buf.at[block(src)], recv.at[block(src)], fwd_send.at[src], fwd_recv.at[src], sec, src
        )

    def ret_copy(peer):
        return remote(
            acts.at[block(peer)], back.at[block(me)], ret_send.at[peer], ret_recv.at[me], sec, peer
        )

    def ret_arrival(src):
        return remote(
            acts.at[block(src)], back.at[block(src)], ret_send.at[src], ret_recv.at[src], sec, src
        )

    def in_plane(plane, visit):
        for s in range(PLANE):
            peer = plane * PLANE + lax.rem(j + s, PLANE)
            if s > 0:
                visit(peer)
            else:
                @pl.when(plane != a)
                def _():
                    visit(peer)

    mid = max(planes // 2, 1)
    side = a // mid

    def visit_order(t):
        across = jnp.where(t < planes - mid, 1, 0)
        base = lax.rem(side + across, planes // mid) * mid
        return base + lax.rem(a + t + 1 - across, mid)

    def group(plane):
        return pl.ds(pl.multiple_of(plane * rows, rows), rows)

    def dispatch(dz, carry):
        plane = visit_order(dz)
        at = (lax.broadcasted_iota(jnp.int32, (rows, tok), 0) + plane * rows).astype(F32)
        placing = jnp.where(slot_row == at, 1.0, 0.0).astype(BF16)
        buf[group(plane), :] = jnp.dot(placing, mixed[...], preferred_element_type=F32).astype(BF16)
        in_plane(plane, lambda peer: fwd_copy(peer).start())
        return carry

    lax.fori_loop(0, planes, dispatch, 0)
    recv[block(me), :] = buf[block(me), :]

    def cnt_wait(k, carry):
        src = lax.rem(me + k, experts)
        remote(cnt.at[src], cnt.at[src], cnt_send.at[k], cnt_recv.at[src], sec, src).wait_recv()
        return carry

    lax.fori_loop(1, experts, cnt_wait, 0)
    get_w.wait()
    counts = cnt[:, 0, :].astype(BF16)
    limit = capacity[0, 0].astype(F32)

    def expert(dz, carry):
        plane = visit_order(dz)
        in_plane(plane, lambda src: fwd_arrival(src).wait_recv())
        act = jnp.maximum(
            jnp.dot(recv[group(plane), :], w_vmem[...], preferred_element_type=F32), 0.0
        )
        row = lax.broadcasted_iota(jnp.int32, (rows, experts), 0)
        source = lax.broadcasted_iota(jnp.int32, (rows, experts), 1)
        lower = jnp.where(source < plane * PLANE + row // cap, 1.0, 0.0).astype(BF16)
        sums = jnp.dot(lower, counts, preferred_element_type=F32)
        mine = lax.broadcasted_iota(jnp.int32, (rows, LANES), 1) == me
        offset = jnp.sum(jnp.where(mine, sums, 0.0), axis=1, keepdims=True)
        rank = offset + (lax.broadcasted_iota(jnp.int32, (rows, 1), 0) % cap).astype(F32)
        kept = jnp.where(rank < limit, 1.0, 0.0)
        acts[group(plane), :] = (act * kept).astype(BF16)
        in_plane(plane, lambda peer: ret_copy(peer).start())
        return carry

    lax.fori_loop(0, planes, expert, 0)
    back[block(me), :] = acts[block(me), :]
    acc[...] = jnp.zeros_like(acc)

    def combine(dz, carry):
        plane = visit_order(dz)
        in_plane(plane, lambda src: ret_arrival(src).wait_recv())
        at = (lax.broadcasted_iota(jnp.int32, (tok, rows), 1) + plane * rows).astype(F32)
        placing = jnp.where(slot_col == at, 1.0, 0.0).astype(BF16)
        acc[...] += jnp.dot(placing, back[group(plane), :], preferred_element_type=F32)
        return carry

    lax.fori_loop(0, planes, combine, 0)
    out[0] = (acc[...] * gate_col).astype(BF16)

    def sent(k, carry):
        peer = lax.rem(me + k, experts)
        cnt_copy(k).wait_send()
        fwd_copy(peer).wait_send()
        ret_copy(peer).wait_send()
        return carry

    lax.fori_loop(1, experts, sent, 0)

    @pl.when(jnp.logical_not(decoding))
    def _():
        for copy in kv:
            copy.wait_send()

    @pl.when(decoding)
    def _():
        for kind in range(2):
            def w_sent(dz, carry):
                for hop in range(4):
                    def done():
                        w_copy(kind, hop, dz, me, a * PLANE + by_x).wait_send()

                    if hop == 0:
                        pl.when(dz > 0)(done)
                    else:
                        done()
                return carry

            lax.fori_loop(0, planes, w_sent, 0)


def shards(
    tokens, gates, routes, capacity, mem_lengths, mem_keys, mem_values, q_weight, out_weight, w_in
):
    sections = lax.axis_size("section")
    experts = lax.axis_size("expert")
    tok, width = tokens.shape[1:]
    hidden = w_in.shape[3]
    span = mem_keys.shape[1]
    cap = max(16, 2 * tok // experts)
    slots = experts * cap
    planes = experts // PLANE
    dma = pltpu.SemaphoreType.DMA
    vmem = pl.BlockSpec(memory_space=pltpu.VMEM)
    smem = pl.BlockSpec(memory_space=pltpu.SMEM)
    hbm = pl.BlockSpec(memory_space=pl.ANY)
    return pl.pallas_call(
        functools.partial(relay, sections, experts, cap),
        out_shape=jax.ShapeDtypeStruct((1, tok, hidden), BF16),
        in_specs=[hbm, vmem, vmem, smem, smem, hbm, hbm, hbm, hbm, hbm],
        out_specs=vmem,
        scratch_shapes=[
            pltpu.VMEM((width, hidden), BF16),
            pltpu.VMEM((tok, width), BF16),
            pltpu.VMEM((2, width, width), BF16),
            pltpu.VMEM((2 * span, width), BF16),
            pltpu.VMEM((2 * span, width), BF16),
            pltpu.VMEM((tok, width), BF16),
            pltpu.VMEM((tok, width), BF16),
            pltpu.VMEM((tok, width), BF16),
            pltpu.VMEM((slots, width), BF16),
            pltpu.VMEM((slots, width), BF16),
            pltpu.VMEM((slots, hidden), BF16),
            pltpu.VMEM((slots, hidden), BF16),
            pltpu.VMEM((tok, hidden), F32),
            pltpu.VMEM((experts, 8, LANES), F32),
            pltpu.SemaphoreType.REGULAR,
            dma((6,)),
            dma((2,)),
            dma((2,)),
            dma((2, 4, planes)),
            dma((2, experts)),
            dma((experts,)),
            dma((experts,)),
            dma((experts,)),
            dma((experts,)),
            dma((experts,)),
            dma((experts,)),
        ],
        compiler_params=pltpu.CompilerParams(
            collective_id=0, has_side_effects=True, vmem_limit_bytes=63 * 1024 * 1024
        ),
        cost_estimate=pl.CostEstimate(
            flops=4 * tok * width * width + 2 * slots * width * hidden,
            bytes_accessed=2 * width * hidden + 8 * width * width,
            transcendentals=HEADS * tok * 2 * span,
        ),
    )(
        tokens, gates, routes.reshape(1, tok), capacity, mem_lengths,
        mem_keys, mem_values, q_weight, out_weight, w_in,
    )


def solution(mesh):
    in_specs = (
        P("section", "expert", None),
        P("section", "expert"),
        P("section", "expert", None),
        P("section", "expert"),
        P("section", "expert"),
        P("section", "expert", None),
        P("section", "expert", None),
        P("section", "expert", None),
        P("section", "expert", None),
        P("section", "expert", None, None),
    )
    out_specs = P("section", "expert", None)
    return jax.shard_map(shards, mesh=mesh, in_specs=in_specs, out_specs=out_specs, check_vma=False)
```
